128 devices in a mesh: dp: 16 (over z, x), tensor: 8 (over y, core).
Axes of the slice: x: 4, y: 4, z: 4, core: 2. Of those that a mesh axis runs over, the one named last changes fastest.
Arguments:
- acts: bfloat16 [49152, 8192], P('dp', 'tensor'), may hold values from -60 to 60
- cotangent: bfloat16 [49152, 2048], P(('dp', 'tensor')), may hold values from -6 to 6
- master: float32 [8192, 2048], P('tensor', 'dp'), may hold values from -0.0625 to 0.0625
- first_moment: float32 [8192, 2048], P('tensor', 'dp'), may hold values from -4 to 4
- second_moment: float32 [8192, 2048], P('tensor', 'dp'), may hold values from 0.01 to 1
Outputs:
- new_master: float32 [8192, 2048], P('tensor', 'dp')
- new_first: float32 [8192, 2048], P('tensor', 'dp')
- new_second: float32 [8192, 2048], P('tensor', 'dp')
- weights: bfloat16 [8192, 2048], P('tensor')
- block_scales: float32 [64, 16], P('tensor')
The draws below stay inside these ranges and needn't reach their ends.
All inputs are finite; a program needn't handle non-finite values.
Results may differ from the reference program's by a relative error of at most 0.02.
Values may be sent and summed in bfloat16 or wider, within the bound.
A program may use at most 192 MiB of HBM per device.

```python
import math
import jax
import jax.numpy as jnp
from jax import lax

D = 8192
BLOCK = 128
KV = 2048
TOKENS = 49152
N_DP = 16


def draw_acts(key, part):
    key = jax.random.fold_in(key, 11)
    first_key = jax.random.fold_in(key, 0)
    ramp = 1.0 + 2.0 * jnp.arange(TOKENS, dtype=jnp.float32) / TOKENS
    values = jnp.clip(jax.random.normal(first_key, (TOKENS, D), jnp.float32), -6.0, 6.0)
    return (values * ramp[:, None]).astype(jnp.bfloat16)


def level_of(key, extent, pieces, smallest, largest):
    loudness = 1.0
    for axis_at, blocks in pieces:
        heights = jax.random.uniform(jax.random.fold_in(jax.random.fold_in(key, 6), axis_at), (blocks,), jnp.float32, smallest / len(pieces), largest / len(pieces))
        loudness = loudness * jnp.repeat(jnp.exp(heights), extent[axis_at] // blocks).reshape((-1,) + (1,) * (len(extent) - 1 - axis_at))
    return loudness


def gaussian(own_key, shape, width, limit, cuts=(), held_as=jnp.bfloat16):
    factor_of = level_of(own_key, shape, cuts, -0.22, 0.18) if cuts else 1.0
    entries = jax.random.normal(own_key, shape, jnp.float32) * width * factor_of
    return jnp.minimum(jnp.maximum(entries, -limit), limit).astype(held_as)


def setup_inputs(seed: int = 0) -> dict:
    key_list = jax.random.split(jax.random.key(seed), 6)
    return {
        "acts": draw_acts(jax.random.fold_in(key_list[5], 71), 0),
        "cotangent": gaussian(key_list[1], (TOKENS, KV), 1.0, 6.0, ((0, 128),)),
        "master": gaussian(key_list[2], (D, KV), D ** -0.5, 0.0625, ((0, 8), (1, 16)), jnp.float32),
        "first_moment": gaussian(key_list[3], (D, KV), 0.5, 4.0, ((0, 8), (1, 16)), jnp.float32),
        "second_moment": jnp.clip(jnp.exp(math.log(1.0) - 4.6051702 * jax.random.uniform(key_list[4], (D, KV), jnp.float32) ** level_of(key_list[4], (D, KV), ((0, 8), (1, 16)), -0.2, 0.2)), 0.01, 1.0),
    }


def widen(small):
    return jnp.repeat(jnp.repeat(small, BLOCK, axis=0), BLOCK, axis=1)

def reference(acts, cotangent, master, first_moment, second_moment):
    groups_x = acts.reshape(N_DP, -1, D)
    groups_y = cotangent.reshape(N_DP, -1, KV)

    def one_group(pair):
        left, right = pair
        return lax.dot_general(left, right, (((0,), (0,)), ((), ())), preferred_element_type=jnp.float32)
    partial_value = lax.map(one_group, (groups_x, groups_y))
    magnitude = jnp.abs(partial_value).reshape(N_DP, D // BLOCK, BLOCK, KV // BLOCK, BLOCK)
    block_scales = lax.optimization_barrier(jnp.max(magnitude, axis=(0, 2, 4))) + 1e-06
    wide_scale = widen(block_scales)
    quantized = (partial_value / wide_scale[None]).astype(jnp.bfloat16)
    quantized = lax.optimization_barrier(quantized)
    summed = lax.optimization_barrier(jnp.sum(quantized.astype(jnp.float32), axis=0))
    gradient = summed * wide_scale / math.sqrt(TOKENS)
    new_first = 0.9 * first_moment + 0.1 * gradient
    new_second = 0.95 * second_moment + 0.05 * gradient * gradient
    first_hat = new_first / (1.0 - 0.9 ** 10)
    second_hat = new_second / (1.0 - 0.95 ** 10)
    new_master = master * (1.0 - 0.01 * 0.1) - 0.01 * first_hat / (jnp.sqrt(second_hat) + 1e-08)
    weights = new_master.astype(jnp.bfloat16)
    return (new_master, new_first, new_second, weights, block_scales)
```

```python
import functools
import math

import jax
import jax.numpy as jnp
from jax import lax
from jax.experimental import pallas as pl
from jax.experimental.pallas import tpu as pltpu
from jax.sharding import PartitionSpec as P

MESH = pl.DeviceIdType.MESH
BLOCK = 128
RING = 4
PAIRS = 8
F32 = jnp.float32
BF16 = jnp.bfloat16


def schedule():
    ops = [("own", 0), ("own", 1), ("turn",)]
    for s in range(PAIRS + 1):
        if s < PAIRS:
            ops += [("near", s)]
            if s + 2 < PAIRS:
                ops += [("own", s + 2)]
        if s >= 1:
            ops += [("far", s - 1)]
            d, odd = (s - 1) // 2, (s - 1) % 2
            if odd:
                if d >= 1:
                    ops += [("w1", d - 1, 0), ("w1", d - 1, 1)]
                ops += [("mm", s - 1, 0), ("r1a", d, 0), ("mm", s - 1, 1), ("r1a", d, 1)]
                if d >= 1:
                    ops += [("w2", d - 1, 0), ("w2", d - 1, 1)]
                ops += [("r1b", d, 0), ("r1b", d, 1)]
            else:
                ops += [("mm", s - 1, 0), ("mm", s - 1, 1)]
                if d >= 1:
                    ops += [("r1c", d - 1, 0), ("r1c", d - 1, 1), ("u", d - 1, 0), ("u", d - 1, 1)]
                if d >= 2:
                    ops += [("w3", d - 2, 0), ("w3", d - 2, 1)]
    last = RING - 1
    ops += [("mx0",)]
    for name in ("r1c", "u", "w1", "w2"):
        ops += [(name, last, 0), (name, last, 1)]
        if name == "r1c":
            ops += [("mx1",)]
        if name == "u":
            ops += [("mx2",)]
    for d in (last - 1, last):
        ops += [("w3", d, 0), ("w3", d, 1)]
    return ops


def kernel(
    token_count,
    acts, cotangent, master, first, second,
    new_master, new_first, new_second, weights, scales,
    plain, turned, cols, part, far_in, near_in, staged, sums_in, held,
    w_in, f_in, s_in, w_out, f_out, s_out,
    peak, peak_x, peak_z, peak_in,
    send, recv, local,
):
    dp, tensor = lax.axis_index("dp"), lax.axis_index("tensor")
    z, x = lax.div(dp, RING), lax.rem(dp, RING)
    y, core = lax.div(tensor, 2), lax.rem(tensor, 2)
    tokens, rows = plain.shape
    share = tokens // (2 * RING)
    half_rows = rows // 2
    quarter = half_rows // 2

    def at(dz=0, dx=0, dy=0, dc=0):
        return (
            lax.rem(z + dz, RING) * RING + lax.rem(x + dx, RING),
            lax.rem(y + dy, RING) * 2 + lax.rem(core + dc, 2),
        )

    counts = {"send": 0, "recv": 0, "local": 0}
    names = {}

    def sem(kind, *key, n=1):
        if (kind, key) not in names:
            names[kind, key] = counts[kind]
            counts[kind] += n
        return names[kind, key]

    drain = []

    def push(ref, key, device, dst=None, recv_at=None, when=None):
        at_recv = sem("recv", *key) if recv_at is None else recv_at
        copy = pltpu.make_async_remote_copy(
            src_ref=ref, dst_ref=ref if dst is None else dst,
            send_sem=send.at[sem("send", *key)], recv_sem=recv.at[at_recv],
            device_id=device, device_id_type=MESH,
        )
        copy.start()
        drain.append((ref, sem("send", *key), when))

    def arrived(ref, key, recv_at=None):
        at_recv = sem("recv", *key) if recv_at is None else recv_at
        pltpu.make_async_remote_copy(
            src_ref=ref, dst_ref=ref, send_sem=send.at[0], recv_sem=recv.at[at_recv],
            device_id=at(dc=1), device_id_type=MESH,
        ).wait_recv()

    def load(src, dst, *key):
        copy = pltpu.make_async_copy(src, dst, local.at[sem("local", *key)])
        copy.start()
        return copy

    def owner_of(d, j):
        return j * RING + (j + d) % RING

    mine = pl.ds(pl.multiple_of(tensor * share, share), share)
    own_loads = []
    for s in range(PAIRS):
        pair = []
        for h in range(2):
            column = owner_of(s // 2, s % 2 * 2 + h) * BLOCK
            pair.append(load(
                cotangent.at[:, pl.ds(column, BLOCK)],
                cols.at[s, mine, pl.ds(h * BLOCK, BLOCK)], "own", s, h,
            ))
        own_loads.append(pair)
    act_loads = [
        load(acts.at[pl.ds(i * share, share)], plain.at[pl.ds(i * share, share)], "acts", i)
        for i in range(2 * RING)
    ]
    state_loads = [
        load(a, b, "state", i) for i, (a, b) in enumerate(((master, w_in), (first, f_in), (second, s_in)))
    ]

    barrier = pltpu.get_barrier_semaphore()
    partners = [at(dy=1), at(dy=3), at(dc=1)]
    partners += [at(dx=i) for i in (1, 2, 3)] + [at(dz=i) for i in (1, 2, 3)]
    for device in partners:
        pl.semaphore_signal(barrier, inc=1, device_id=device, device_id_type=MESH)
    pl.semaphore_wait(barrier, len(partners))

    def token_rows(dy, dc=0, part_of=None):
        start = (lax.rem(y + dy, RING) * 2 + lax.rem(core + dc, 2)) * share
        size = share
        if part_of is not None:
            size = share // 2
            start = start + part_of * size
        return pl.ds(pl.multiple_of(start, size), size)

    def own(s):
        for copy in own_loads[s]:
            copy.wait()
        block = cols.at[s, token_rows(0)]
        push(block, ("g", s, "+"), at(dy=1))
        push(block, ("g", s, "-"), at(dy=3))
        push(block, ("g", s, "c", 0), at(dc=1))

    def near(s):
        for sign, dy, piece, to in (("+", 3, 0, 1), ("-", 1, 1, 3)):
            arrived(cols.at[s, token_rows(dy)], ("g", s, sign))
            push(cols.at[s, token_rows(dy, 0, piece)], ("gf", s, sign), at(dy=to))
            push(cols.at[s, token_rows(dy)], ("g", s, "c", dy), at(dc=1))

    def far(s):
        for sign, piece in (("+", 0), ("-", 1)):
            block = cols.at[s, token_rows(2, 0, piece)]
            arrived(block, ("gf", s, sign))
            push(block, ("gfc", s, sign), at(dc=1))
        for dy in (0, 1, 3):
            arrived(cols.at[s, token_rows(dy, 1)], ("g", s, "c", dy))
        for sign, piece in (("+", 0), ("-", 1)):
            arrived(cols.at[s, token_rows(2, 1, piece)], ("gfc", s, sign))

    def turn():
        for i, copy in enumerate(act_loads):
            copy.wait()
            for k in range(rows // 256):
                turned[pl.ds(k * 256, 256), pl.ds(i * share, share)] = (
                    plain[pl.ds(i * share, share), pl.ds(k * 256, 256)].T
                )
        peak[...] = jnp.zeros_like(peak)

    row_id = lax.broadcasted_iota(jnp.int32, peak.shape, 0)
    lane_id = lax.broadcasted_iota(jnp.int32, peak.shape, 1)

    def mm(s, t):
        d = s // 2

        def step(i, carry):
            start = pl.multiple_of(t * half_rows + i * 256, 256)
            value = jnp.dot(turned[pl.ds(start, 256), :], cols[s], preferred_element_type=F32)
            top = peak[...]
            for h in range(2):
                j = s % 2 * 2 + h
                block = value[:, h * BLOCK:(h + 1) * BLOCK]
                part[d, j, pl.ds(start, 256), :] = block.astype(BF16)
                for r in range(2):
                    largest = jnp.max(jnp.abs(block[r * BLOCK:(r + 1) * BLOCK]), axis=(0, 1), keepdims=True)
                    here = (row_id == t * (half_rows // BLOCK) + i * 2 + r) & (lane_id == owner_of(d, j))
                    top = jnp.where(here, largest, top)
            peak[...] = top
            return carry

        lax.fori_loop(0, half_rows // 256, step, 0)

    def first_axis(t, delta):
        return at(dx=delta) if t == 0 else at(dz=delta)

    def second_axis(t, delta):
        return at(dz=delta) if t == 0 else at(dx=delta)

    def target(d, t, delta):
        return lax.rem(x + delta - d + RING, RING) if t == 0 else lax.rem(z + delta, RING)

    def from_owner(d, t):
        return lax.rem(z - x + d + RING, RING) if t == 0 else lax.rem(x - z - d + 2 * RING, RING)

    def rows_of(t, piece=None):
        if piece is None:
            return pl.ds(t * half_rows, half_rows)
        return pl.ds(t * half_rows + piece * quarter, quarter)

    def r1a(d, t):
        distant = target(d, t, 2)
        for sign, piece, to in (("+", 0, 1), ("-", 1, 3)):
            push(part.at[d, distant, rows_of(t, piece)], ("r1f", d, t, sign), first_axis(t, to), dst=far_in.at[d, t, piece])
        for sign, piece, to in (("+", 0, 1), ("-", 1, 3)):
            push(
                part.at[d, target(d, t, to), rows_of(t, 1 - piece)], ("r1i", d, t, sign), first_axis(t, to),
                dst=near_in.at[d, t, piece, pl.ds((1 - piece) * quarter, quarter)],
            )

    def r1b(d, t):
        for sign, piece, to in (("+", 0, 1), ("-", 1, 3)):
            arrived(far_in.at[d, t, piece], ("r1f", d, t, sign))
            block = part.at[d, target(d, t, to), rows_of(t, piece)]
            block[...] = (block[...].astype(F32) + far_in[d, t, piece].astype(F32)).astype(BF16)
            push(
                block, ("r1d", d, t, sign), first_axis(t, to),
                dst=near_in.at[d, t, piece, pl.ds(piece * quarter, quarter)],
            )

    def r1c(d, t):
        for sign, piece in (("+", 0), ("-", 1)):
            arrived(near_in.at[d, t, piece, pl.ds((1 - piece) * quarter, quarter)], ("r1i", d, t, sign))
            arrived(near_in.at[d, t, piece, pl.ds(piece * quarter, quarter)], ("r1d", d, t, sign))
        total = part[d, target(d, t, 0), rows_of(t), :].astype(F32)
        total = total + near_in[d, t, 0].astype(F32) + near_in[d, t, 1].astype(F32)
        staged[d, t] = total.astype(BF16)
        delta = from_owner(d, t)
        away = delta != 0
        block = staged.at[d, t]
        base = sem("recv", "r2", t, n=3)

        @pl.when(away)
        def _():
            push(
                block, ("r2", d, t), second_axis(t, RING - delta),
                dst=sums_in.at[t, delta - 1], recv_at=base + delta - 1, when=away,
            )

    def owned(t, owner):
        return held.at[rows_of(t), pl.ds(pl.multiple_of(owner * BLOCK, BLOCK), BLOCK)]

    def u(d, t):
        delta = from_owner(d, t)
        base = sem("recv", "r2", t, n=3)
        block = owned(t, dp)
        at_owner = delta == 0

        @pl.when(at_owner)
        def _():
            if t == 0:
                for copy in state_loads:
                    copy.wait()
            total = staged[d, t].astype(F32)
            for i in range(3):
                arrived(sums_in.at[t, i], None, recv_at=base + i)
                total = total + sums_in[t, i].astype(F32)
            here = rows_of(t)
            gradient = total * (1.0 / math.sqrt(token_count))
            f_new = 0.9 * f_in[here, :] + 0.1 * gradient
            s_new = 0.95 * s_in[here, :] + 0.05 * gradient * gradient
            f_hat = f_new / (1.0 - 0.9**10)
            s_hat = s_new / (1.0 - 0.95**10)
            w_new = w_in[here, :] * (1.0 - 0.01 * 0.1) - 0.01 * f_hat / (jnp.sqrt(s_hat) + 1e-08)
            f_out[here, :] = f_new
            s_out[here, :] = s_new
            w_out[here, :] = w_new
            block[...] = w_new.astype(BF16)
            for i in (1, 2, 3):
                push(block, ("w1", d, t, i), second_axis(t, i), recv_at=sem("recv", "w1", d, t), when=at_owner)

    def block_at(d, t, delta):
        if t == 0:
            ox = lax.rem(x + delta, RING)
            oz = lax.rem(ox - d + RING, RING)
        else:
            oz = lax.rem(z + delta, RING)
            ox = lax.rem(oz + d, RING)
        return oz * RING + ox

    def w1(d, t):
        block = owned(t, block_at(d, t, 0))

        @pl.when(from_owner(d, t) != 0)
        def _():
            arrived(block, None, recv_at=sem("recv", "w1", d, t))

        for sign, to in (("+", 1), ("-", 3)):
            push(block, ("w2", d, t, sign), first_axis(t, to))

    def half_block(d, t, delta, piece):
        owner = block_at(d, t, delta)
        return held.at[rows_of(t, piece), pl.ds(pl.multiple_of(owner * BLOCK, BLOCK), BLOCK)]

    def w2(d, t):
        for sign, piece, frm, to in (("+", 0, 3, 1), ("-", 1, 1, 3)):
            arrived(owned(t, block_at(d, t, frm)), ("w2", d, t, sign))
            push(half_block(d, t, frm, piece), ("w2f", d, t, sign), first_axis(t, to))

    out_copies = []

    def w3(d, t):
        for sign, piece in (("+", 0), ("-", 1)):
            arrived(half_block(d, t, 2, piece), ("w2f", d, t, sign))
        for j in range(RING):
            place = (rows_of(t), pl.ds(owner_of(d, j) * BLOCK, BLOCK))
            out_copies.append(load(held.at[place], weights.at[place], "out", d, t, j))

    def mx0():
        peak_x[...] = peak[...]
        for i in (1, 2, 3):
            push(peak_x, ("mx", i), at(dx=i), dst=peak_in.at[i - 1])

    def mx1():
        top = peak_x[...]
        for i in (1, 2, 3):
            arrived(peak_in.at[i - 1], ("mx", i))
            top = jnp.maximum(top, peak_in[i - 1])
        peak_z[...] = top
        for i in (1, 2, 3):
            push(peak_z, ("mz", i), at(dz=i), dst=peak_in.at[i + 2])

    def mx2():
        top = peak_z[...]
        for i in (1, 2, 3):
            arrived(peak_in.at[i + 2], ("mz", i))
            top = jnp.maximum(top, peak_in[i + 2])
        scales[...] = top[:, : scales.shape[1]] + 1e-06

    steps = {f.__name__: f for f in (own, near, far, turn, mm, r1a, r1b, r1c, u, w1, w2, w3, mx0, mx1, mx2)}
    for name, *args in schedule():
        steps[name](*args)

    for i, (a, b) in enumerate(((w_out, new_master), (f_out, new_first), (s_out, new_second))):
        out_copies.append(load(a, b, "state out", i))

    def sent(ref, index):
        pltpu.make_async_remote_copy(
            src_ref=ref, dst_ref=ref, send_sem=send.at[index], recv_sem=recv.at[0],
            device_id=at(dc=1), device_id_type=MESH,
        ).wait_send()

    for ref, index, when in drain:
        if when is None:
            sent(ref, index)
        else:
            pl.when(when)(functools.partial(sent, ref, index))
    for copy in out_copies:
        copy.wait()


def body(acts, cotangent, master, first_moment, second_moment):
    tokens, rows = acts.shape
    columns = cotangent.shape[1]
    half = rows // 2
    state = jax.ShapeDtypeStruct(master.shape, F32)
    anywhere = pl.BlockSpec(memory_space=pl.ANY)
    vmem = pltpu.VMEM
    scratch = [
        vmem((tokens, rows), BF16),
        vmem((rows, tokens), BF16),
        vmem((PAIRS, tokens, 2 * BLOCK), BF16),
        vmem((RING, RING, rows, BLOCK), BF16),
        vmem((RING, 2, 2, half // 2, BLOCK), BF16),
        vmem((RING, 2, 2, half, BLOCK), BF16),
        vmem((RING, 2, half, BLOCK), BF16),
        vmem((2, 3, half, BLOCK), BF16),
        vmem((rows, columns), BF16),
    ]
    scratch += [vmem(master.shape, F32)] * 6
    scratch += [vmem((8, BLOCK), F32)] * 3 + [vmem((6, 8, BLOCK), F32)]
    scratch += [
        pltpu.SemaphoreType.DMA((200,)),
        pltpu.SemaphoreType.DMA((200,)),
        pltpu.SemaphoreType.DMA((64,)),
    ]
    return pl.pallas_call(
        functools.partial(kernel, tokens * lax.axis_size("dp")),
        out_shape=[
            state, state, state,
            jax.ShapeDtypeStruct((rows, columns), BF16),
            jax.ShapeDtypeStruct((rows // BLOCK, columns // BLOCK), F32),
        ],
        in_specs=[anywhere] * 5,
        out_specs=[anywhere] * 4 + [pl.BlockSpec(memory_space=pltpu.VMEM)],
        scratch_shapes=scratch,
        compiler_params=pltpu.CompilerParams(
            collective_id=0, has_side_effects=True, vmem_limit_bytes=62 * 2**20
        ),
    )(acts, cotangent, master, first_moment, second_moment)


def solution(mesh):
    in_specs = (
        P("dp", "tensor"),
        P(("dp", "tensor"), None),
        P("tensor", "dp"),
        P("tensor", "dp"),
        P("tensor", "dp"),
    )
    out_specs = (
        P("tensor", "dp"),
        P("tensor", "dp"),
        P("tensor", "dp"),
        P("tensor", None),
        P("tensor", None),
    )
    return jax.shard_map(body, mesh=mesh, in_specs=in_specs, out_specs=out_specs, check_vma=False)
```

```python
import functools
import math

import jax
import jax.numpy as jnp
from jax import lax
from jax.experimental import pallas as pl
from jax.experimental.pallas import tpu as pltpu
from jax.sharding import PartitionSpec as P

MESH = pl.DeviceIdType.MESH
BLOCK = 128
RING = 4
PAIRS = 8
F32 = jnp.float32
BF16 = jnp.bfloat16


LAST = PAIRS - 1


def schedule():
    ops = [("own", 0), ("own", 1), ("hand",), ("turn",)]
    lag = {"r1c": 2, "u": 3, "w1": 4, "w2": 5}
    for i in range(PAIRS + 5):
        if i < PAIRS:
            ops.append(("near", i))
            if i + 2 < PAIRS:
                ops.append(("own", i + 2))
        s = i - 1
        if 0 <= s < PAIRS:
            ops.append(("far", s))
            for t in range(2):
                ops += [("mm", s, t), ("r1", s, t)]
        if s == LAST:
            ops.append(("mx0",))
        for name, back in lag.items():
            s = i - back
            if 0 <= s < PAIRS:
                ops += [(name, s, 0), (name, s, 1)]
                if s == LAST and name == "u":
                    ops.append(("mx1",))
                if s == LAST and name == "w1":
                    ops += [("mx2",), ("states",)]
    ops += [("w3", s, t) for s in range(PAIRS) for t in range(2)]
    return ops


def adamw(master, first, second, gradient):
    f_new = 0.9 * first + 0.1 * gradient
    s_new = 0.95 * second + 0.05 * gradient * gradient
    f_hat = f_new / (1.0 - 0.9**10)
    s_hat = s_new / (1.0 - 0.95**10)
    w_new = master * (1.0 - 0.01 * 0.1) - 0.01 * f_hat / (jnp.sqrt(s_hat) + 1e-08)
    return w_new, f_new, s_new


def kernel(
    token_count,
    acts, cotangent, master, first, second,
    w_out, f_out, s_out, held, scales,
    plain, turned, cols, part, r1_in, once, r2_in, grads, grad_in,
    w_in, f_in, s_in, narrow, narrow_in,
    peak, peak_x, peak_z, peak_in,
    send, recv, local,
):
    dp, tensor = lax.axis_index("dp"), lax.axis_index("tensor")
    z, x = lax.div(dp, RING), lax.rem(dp, RING)
    y, core = lax.div(tensor, 2), lax.rem(tensor, 2)
    tokens, rows = plain.shape
    share = tokens // (2 * RING)
    half = rows // 2
    quarter = half // RING
    piece = quarter // RING

    def at(dz=0, dx=0, dy=0, dc=0):
        return (
            lax.rem(z + dz, RING) * RING + lax.rem(x + dx, RING),
            lax.rem(y + dy, RING) * 2 + lax.rem(core + dc, 2),
        )

    counts = {"send": 0, "recv": 0, "local": 0}
    names = {}

    def sem(kind, *key):
        if (kind, key) not in names:
            names[kind, key] = counts[kind]
            counts[kind] += 1
        return names[kind, key]

    def push(ref, key, device, dst=None):
        pltpu.make_async_remote_copy(
            src_ref=ref, dst_ref=ref if dst is None else dst,
            send_sem=send.at[sem("send", key[0])], recv_sem=recv.at[sem("recv", *key)],
            device_id=device, device_id_type=MESH,
        ).start()

    def arrived(ref, *key):
        pltpu.make_async_remote_copy(
            src_ref=ref, dst_ref=ref, send_sem=send.at[0], recv_sem=recv.at[sem("recv", *key)],
            device_id=at(dc=1), device_id_type=MESH,
        ).wait_recv()

    def sent(ref, kind, times=1):
        for _ in range(times):
            pltpu.make_async_remote_copy(
                src_ref=ref, dst_ref=ref, send_sem=send.at[sem("send", kind)], recv_sem=recv.at[0],
                device_id=at(dc=1), device_id_type=MESH,
            ).wait_send()

    def load(src, dst, *key):
        copy = pltpu.make_async_copy(src, dst, local.at[sem("local", *key)])
        copy.start()
        return copy

    def owner_of(s, h):
        d, j = s // 2, s % 2 + 2 * h
        return j * RING + (j + d) % RING

    barrier = pltpu.get_barrier_semaphore()
    partners = [at(dy=1), at(dy=3), at(dc=1)]
    partners += [at(dz=i // RING, dx=i % RING) for i in range(1, RING * RING)]
    for device in partners:
        pl.semaphore_signal(barrier, inc=1, device_id=device, device_id_type=MESH)

    mine = pl.ds(pl.multiple_of(tensor * share, share), share)
    own_loads = [
        [
            load(
                cotangent.at[:, pl.ds(owner_of(s, h) * BLOCK, BLOCK)],
                cols.at[s, mine, pl.ds(h * BLOCK, BLOCK)], "own", s, h,
            )
            for h in range(2)
        ]
        for s in range(PAIRS)
    ]
    state_loads = [
        load(a, b, "state", i) for i, (a, b) in enumerate(((master, w_in), (first, f_in), (second, s_in)))
    ]
    act_loads = [
        load(acts.at[pl.ds(i * share, share)], plain.at[pl.ds(i * share, share)], "acts", i)
        for i in range(2 * RING)
    ]

    pl.semaphore_wait(barrier, len(partners))

    def token_rows(dy, part_of=None):
        start = (lax.rem(y + dy, RING) * 2 + core) * share
        size = share
        if part_of is not None:
            size = share // 2
            start = start + part_of * size
        return pl.ds(pl.multiple_of(start, size), size)

    def own(s):
        for copy in own_loads[s]:
            copy.wait()
        block = cols.at[s, token_rows(0)]
        push(block, ("g", s, "+"), at(dy=1))
        push(block, ("g", s, "-"), at(dy=3))
        push(block, ("g", s, "c"), at(dc=1))

    def near(s):
        for sign, dy, k, to in (("+", 3, 0, 1), ("-", 1, 1, 3)):
            arrived(cols.at[s, token_rows(dy)], "g", s, sign)
            push(cols.at[s, token_rows(dy, k)], ("gf", s), at(dy=to))
            push(cols.at[s, token_rows(dy)], ("g", s, "c"), at(dc=1))

    def far(s):
        block = cols.at[s, token_rows(2)]
        arrived(block, "gf", s)
        push(block, ("g", s, "c"), at(dc=1))
        arrived(cols.at[s, pl.ds(0, tokens // 2)], "g", s, "c")

    def turn():
        for i, copy in enumerate(act_loads):
            copy.wait()
            for k in range(rows // 256):
                turned[pl.ds(k * 256, 256), pl.ds(i * share, share)] = (
                    plain[pl.ds(i * share, share), pl.ds(k * 256, 256)].T
                )
        peak[...] = jnp.zeros_like(peak)

    row_id = lax.broadcasted_iota(jnp.int32, peak.shape, 0)
    lane_id = lax.broadcasted_iota(jnp.int32, peak.shape, 1)

    def mm(s, t):
        def step(i, carry):
            start = pl.multiple_of(t * half + i * 256, 256)
            value = jnp.dot(turned[pl.ds(start, 256), :], cols[s], preferred_element_type=F32)
            part[s, pl.ds(start, 256), :] = value.astype(BF16)
            top = peak[...]
            for h in range(2):
                for r in range(2):
                    block = value[r * BLOCK:(r + 1) * BLOCK, h * BLOCK:(h + 1) * BLOCK]
                    largest = jnp.max(jnp.abs(block), axis=(0, 1), keepdims=True)
                    here = (row_id == t * (half // BLOCK) + i * 2 + r) & (lane_id == owner_of(s, h))
                    top = jnp.where(here, largest, top)
            peak[...] = top
            return carry

        lax.fori_loop(0, half // 256, step, 0)

    def along(t, axis, delta):
        return at(dx=delta) if t == axis else at(dz=delta)

    def quarter_rows(t, delta=0):
        place = lax.rem((x if t == 0 else z) + delta, RING)
        return pl.ds(pl.multiple_of(t * half + place * quarter, quarter), quarter)

    def piece_of(t, delta=0):
        place = lax.rem((z if t == 0 else x) + delta, RING)
        return pl.ds(pl.multiple_of(place * piece, piece), piece)

    def piece_rows(t):
        a, b = (x, z) if t == 0 else (z, x)
        return pl.ds(pl.multiple_of(t * half + a * quarter + b * piece, piece), piece)

    def hand():
        for copy in state_loads:
            copy.wait()
        for i, ref in enumerate((w_in, f_in, s_in)):
            narrow[i] = ref[...].astype(BF16)
        for t in range(2):
            narrow_in[t, dp] = narrow[:, piece_rows(t), :]
            for delta in range(1, RING * RING):
                dz, dx = delta // RING, delta % RING
                a, b = lax.rem(x + dx, RING), lax.rem(z + dz, RING)
                if t == 1:
                    a, b = b, a
                here = pl.ds(pl.multiple_of(t * half + a * quarter + b * piece, piece), piece)
                push(narrow.at[:, here], ("hand",), at(dz=dz, dx=dx), dst=narrow_in.at[t, dp])

    def r1(s, t):
        for delta in (1, 3, 2):
            push(part.at[s, quarter_rows(t, delta)], ("r1", s, t), along(t, 0, delta), dst=r1_in.at[s, t, delta - 1])

    def r1c(s, t):
        arrived(r1_in.at[s, t], "r1", s, t)
        total = part[s, quarter_rows(t), :].astype(F32)
        for i in range(RING - 1):
            total = total + r1_in[s, t, i].astype(F32)
        once[s, t] = total.astype(BF16)
        for delta in (1, 3, 2):
            push(once.at[s, t, piece_of(t, delta)], ("r2", s, t), along(t, 1, delta), dst=r2_in.at[s, t, delta - 1])

    def u(s, t):
        if (s, t) == (0, 0):
            arrived(narrow_in.at[:, pl.ds(0, RING * RING - 1)], "hand")
        arrived(r2_in.at[s, t], "r2", s, t)
        total = once[s, t, piece_of(t), :].astype(F32)
        for i in range(RING - 1):
            total = total + r2_in[s, t, i].astype(F32)
        total = total.astype(BF16)
        for h in range(2):
            owner = owner_of(s, h)
            block = total[:, h * BLOCK:(h + 1) * BLOCK]
            grads[s, t, h] = block
            source = grads.at[s, t, h]
            place = grad_in.at[piece_rows(t)]

            @pl.when(dp != owner)
            def _():
                push(source, ("grad",), (owner, tensor), dst=place)

            @pl.when(dp == owner)
            def _():
                place[...] = source[...]

            state = [narrow_in[t, owner, i].astype(F32) for i in range(3)]
            gradient = block.astype(F32) * (1.0 / math.sqrt(token_count))
            held[s, piece_rows(t), h * BLOCK:(h + 1) * BLOCK] = adamw(*state, gradient)[0].astype(BF16)
        for delta in (1, 3, 2):
            push(held.at[s, piece_rows(t)], ("w1", s, t), along(t, 1, delta))

    def w1(s, t):
        arrived(held.at[s, pl.ds(0, 3 * piece)], "w1", s, t)
        for delta in (1, 3):
            push(held.at[s, quarter_rows(t)], ("w2", s, t), along(t, 0, delta))

    def w2(s, t):
        arrived(held.at[s, pl.ds(0, 2 * quarter)], "w2", s, t)
        for k, to in ((0, 1), (1, 3)):
            start = quarter_rows(t, RING - to).start + k * (quarter // 2)
            block = held.at[s, pl.ds(pl.multiple_of(start, quarter // 2), quarter // 2)]
            push(block, ("w2f", s, t), along(t, 0, to))

    def w3(s, t):
        arrived(held.at[s, pl.ds(0, quarter)], "w2f", s, t)

    def states():
        arrived(grad_in.at[pl.ds(0, rows - 2 * piece)], "grad")
        gradient = grad_in[...].astype(F32) * (1.0 / math.sqrt(token_count))
        w_out[...], f_out[...], s_out[...] = adamw(w_in[...], f_in[...], s_in[...], gradient)

    def mx0():
        peak_x[...] = peak[...]
        for i in (1, 2, 3):
            push(peak_x, ("mx",), at(dx=i), dst=peak_in.at[i - 1])

    def mx1():
        arrived(peak_in.at[pl.ds(0, 3)], "mx")
        top = jnp.maximum(jnp.maximum(peak_in[0], peak_in[1]), jnp.maximum(peak_in[2], peak_x[...]))
        peak_z[...] = top
        for i in (1, 2, 3):
            push(peak_z, ("mz",), at(dz=i), dst=peak_in.at[i + 2])

    def mx2():
        arrived(peak_in.at[pl.ds(3, 3)], "mz")
        top = jnp.maximum(jnp.maximum(peak_in[3], peak_in[4]), jnp.maximum(peak_in[5], peak_z[...]))
        scales[...] = top[:, : scales.shape[1]] + 1e-06

    steps = {f.__name__: f for f in (own, near, far, hand, turn, mm, r1, r1c, u, w1, w2, w3, states, mx0, mx1, mx2)}
    for name, *args in schedule():
        steps[name](*args)

    sent(cols.at[:, pl.ds(0, 6 * share)], "g")
    sent(cols.at[:, pl.ds(0, share)], "gf")
    sent(narrow_in.at[:, pl.ds(0, RING * RING - 1)], "hand")
    sent(r1_in, "r1")
    sent(r2_in, "r2")
    sent(grad_in.at[pl.ds(0, rows - 2 * piece)], "grad")
    sent(held.at[:, pl.ds(0, 6 * piece)], "w1")
    sent(held.at[:, pl.ds(0, 4 * quarter)], "w2")
    sent(held.at[:, pl.ds(0, 2 * quarter)], "w2f")
    sent(peak_in.at[pl.ds(0, 3)], "mx")
    sent(peak_in.at[pl.ds(3, 3)], "mz")


def flush(*refs):
    count = (len(refs) - 1) // 2
    ins, outs, sems = refs[:count], refs[count:-1], refs[-1]
    copies = []

    def move(src, dst):
        copies.append(pltpu.make_async_copy(src, dst, sems.at[len(copies)]))
        copies[-1].start()

    for s in range(PAIRS):
        for h in range(2):
            j = s % 2 + 2 * h
            owner = j * RING + (j + s // 2) % RING
            move(ins[3].at[s, :, pl.ds(h * BLOCK, BLOCK)], outs[3].at[:, pl.ds(owner * BLOCK, BLOCK)])
    for i in (0, 1, 2, 4):
        move(ins[i], outs[i])
    for copy in copies:
        copy.wait()


def body(acts, cotangent, master, first_moment, second_moment):
    tokens, rows = acts.shape
    columns = cotangent.shape[1]
    state = pltpu.VMEM(master.shape, F32)
    anywhere = pl.BlockSpec(memory_space=pl.ANY)
    vmem = pltpu.VMEM
    quarter = rows // 2 // RING
    piece = quarter // RING
    scratch = [
        vmem((tokens, rows), BF16),
        vmem((rows, tokens), BF16),
        vmem((PAIRS, tokens, 2 * BLOCK), BF16),
        vmem((PAIRS, rows, 2 * BLOCK), BF16),
        vmem((PAIRS, 2, RING - 1, quarter, 2 * BLOCK), BF16),
        vmem((PAIRS, 2, quarter, 2 * BLOCK), BF16),
        vmem((PAIRS, 2, RING - 1, piece, 2 * BLOCK), BF16),
        vmem((PAIRS, 2, 2, piece, BLOCK), BF16),
        vmem(master.shape, BF16),
    ]
    scratch += [vmem(master.shape, F32)] * 3
    scratch += [vmem((3,) + master.shape, BF16), vmem((2, RING * RING, 3, piece, BLOCK), BF16)]
    scratch += [vmem((8, BLOCK), F32)] * 3 + [vmem((6, 8, BLOCK), F32)]
    scratch += [
        pltpu.SemaphoreType.DMA((12,)),
        pltpu.SemaphoreType.DMA((128,)),
        pltpu.SemaphoreType.DMA((32,)),
    ]
    results = pl.pallas_call(
        functools.partial(kernel, tokens * lax.axis_size("dp")),
        out_shape=[
            state, state, state,
            vmem((PAIRS, rows, 2 * BLOCK), BF16),
            vmem((rows // BLOCK, columns // BLOCK), F32),
        ],
        in_specs=[anywhere] * 5,
        out_specs=[pl.BlockSpec(memory_space=pltpu.VMEM)] * 5,
        scratch_shapes=scratch,
        compiler_params=pltpu.CompilerParams(
            collective_id=0, has_side_effects=True, vmem_limit_bytes=50 * 2**20
        ),
    )(acts, cotangent, master, first_moment, second_moment)
    shapes = [a.shape for a in results]
    shapes[3] = (rows, columns)
    return pl.pallas_call(
        flush,
        out_shape=[jax.ShapeDtypeStruct(shape, a.dtype) for shape, a in zip(shapes, results)],
        in_specs=[anywhere] * len(results),
        out_specs=[anywhere] * len(results),
        scratch_shapes=[pltpu.SemaphoreType.DMA((2 * PAIRS + 4,))],
        compiler_params=pltpu.CompilerParams(vmem_limit_bytes=2**20),
    )(*results)


def solution(mesh):
    in_specs = (
        P("dp", "tensor"),
        P(("dp", "tensor"), None),
        P("tensor", "dp"),
        P("tensor", "dp"),
        P("tensor", "dp"),
    )
    out_specs = (
        P("tensor", "dp"),
        P("tensor", "dp"),
        P("tensor", "dp"),
        P("tensor", None),
        P("tensor", None),
    )
    return jax.shard_map(body, mesh=mesh, in_specs=in_specs, out_specs=out_specs, check_vma=False)
```

```python
import functools
import math

import jax
import jax.numpy as jnp
from jax import lax
from jax.experimental import pallas as pl
from jax.experimental.pallas import tpu as pltpu
from jax.sharding import PartitionSpec as P

MESH = pl.DeviceIdType.MESH
BLOCK = 128
RING = 4
PAIRS = 8
F32 = jnp.float32
BF16 = jnp.bfloat16


CHUNKS = [(s, (0, 1)) for s in range(PAIRS)]
LAST = len(CHUNKS) - 1
DIRECT = LAST


def schedule():
    ops = [("own", 0), ("own", 1), ("hand",), ("turn",)]

    def both(name, c):
        return [(name, c, 0), (name, c, 1)] if 0 <= c <= LAST else []

    for i in range(LAST + 1):
        ops.append(("near", i))
        if i + 2 <= LAST:
            ops.append(("own", i + 2))
        if i >= 1:
            ops.append(("far", i - 1))
            for t in range(2):
                ops += [("mm", i - 1, t), ("r1", i - 1, t)]
        ops += both("r1c", i - 2) + both("u", i - 3) + both("w1", i - 4) + both("w2", i - 5)
    ops += both("mm_near", LAST) + [("far", LAST)]
    for t in range(2):
        ops += [("mm_far", LAST, t), ("r1", LAST, t)]
    ops += both("late", LAST) + [("mx0",)]
    ops += both("r1c", LAST - 1) + both("u", LAST - 2) + both("w1", LAST - 3) + both("w2", LAST - 4)
    ops += both("r1c", LAST) + [("mx1",)] + both("u", LAST - 1) + both("w1", LAST - 2) + both("w2", LAST - 3)
    ops += both("u", LAST) + [("mx2",)] + both("w1", LAST - 1) + both("w2", LAST - 2)
    ops += both("w1", LAST) + both("w2", LAST - 1) + [("states",)] + both("w2", LAST)
    for c in range(LAST + 1):
        ops += both("w3", c)
    return ops


def adamw(master, first, second, gradient):
    f_new = 0.9 * first + 0.1 * gradient
    s_new = 0.95 * second + 0.05 * gradient * gradient
    f_hat = f_new / (1.0 - 0.9**10)
    s_hat = s_new / (1.0 - 0.95**10)
    w_new = master * (1.0 - 0.01 * 0.1) - 0.01 * f_hat / (jnp.sqrt(s_hat) + 1e-08)
    return w_new, f_new, s_new


def kernel(
    token_count,
    acts, cotangent, master, first, second,
    w_out, f_out, s_out, held, scales,
    plain, turned, cols, early, part, r1_in, once, r2_in, grads, grad_in,
    w_in, f_in, s_in, narrow, narrow_in,
    peak, peak_x, peak_z, peak_in,
    send, recv, local,
):
    dp, tensor = lax.axis_index("dp"), lax.axis_index("tensor")
    z, x = lax.div(dp, RING), lax.rem(dp, RING)
    y, core = lax.div(tensor, 2), lax.rem(tensor, 2)
    tokens, rows = plain.shape
    share = tokens // (2 * RING)
    half = rows // 2
    quarter = half // RING
    piece = quarter // RING

    def at(dz=0, dx=0, dy=0, dc=0):
        return (
            lax.rem(z + dz, RING) * RING + lax.rem(x + dx, RING),
            lax.rem(y + dy, RING) * 2 + lax.rem(core + dc, 2),
        )

    counts = {"send": 0, "recv": 0, "local": 0}
    names = {}

    def sem(kind, *key):
        if (kind, key) not in names:
            names[kind, key] = counts[kind]
            counts[kind] += 1
        return names[kind, key]

    def push(ref, key, device, dst=None):
        pltpu.make_async_remote_copy(
            src_ref=ref, dst_ref=ref if dst is None else dst,
            send_sem=send.at[sem("send", key[0])], recv_sem=recv.at[sem("recv", *key)],
            device_id=device, device_id_type=MESH,
        ).start()

    def arrived(ref, *key):
        pltpu.make_async_remote_copy(
            src_ref=ref, dst_ref=ref, send_sem=send.at[0], recv_sem=recv.at[sem("recv", *key)],
            device_id=at(dc=1), device_id_type=MESH,
        ).wait_recv()

    def sent(ref, kind, times=1):
        for _ in range(times):
            pltpu.make_async_remote_copy(
                src_ref=ref, dst_ref=ref, send_sem=send.at[sem("send", kind)], recv_sem=recv.at[0],
                device_id=at(dc=1), device_id_type=MESH,
            ).wait_send()

    def load(src, dst, *key):
        copy = pltpu.make_async_copy(src, dst, local.at[sem("local", *key)])
        copy.start()
        return copy

    def owner_of(s, h):
        d, j = s // 2, s % 2 + 2 * h
        return j * RING + (j + d) % RING

    barrier = pltpu.get_barrier_semaphore()
    partners = [at(dy=1), at(dy=3), at(dc=1)]
    partners += [at(dz=i // RING, dx=i % RING) for i in range(1, RING * RING)]
    for device in partners:
        pl.semaphore_signal(barrier, inc=1, device_id=device, device_id_type=MESH)

    mine = pl.ds(pl.multiple_of(tensor * share, share), share)
    own_loads = [
        [
            load(
                cotangent.at[:, pl.ds(owner_of(s, h) * BLOCK, BLOCK)],
                cols.at[s, mine, pl.ds(h * BLOCK, BLOCK)], "own", s, h,
            )
            for h in range(2)
        ]
        for s in range(PAIRS)
    ]
    state_loads = [
        load(a, b, "state", i) for i, (a, b) in enumerate(((master, w_in), (first, f_in), (second, s_in)))
    ]
    act_loads = [
        load(acts.at[pl.ds(i * share, share)], plain.at[pl.ds(i * share, share)], "acts", i)
        for i in range(2 * RING)
    ]

    pl.semaphore_wait(barrier, len(partners))

    def token_rows(dy, part_of=None):
        start = (lax.rem(y + dy, RING) * 2 + core) * share
        size = share
        if part_of is not None:
            size = share // 2
            start = start + part_of * size
        return pl.ds(pl.multiple_of(start, size), size)

    def lanes(c):
        return pl.ds(CHUNKS[c][1][0] * BLOCK, len(CHUNKS[c][1]) * BLOCK)

    def own(c):
        s, halves = CHUNKS[c]
        for h in halves:
            own_loads[s][h].wait()
        block = cols.at[s, token_rows(0), lanes(c)]
        push(block, ("g", c, "+"), at(dy=1))
        push(block, ("g", c, "-"), at(dy=3))
        push(block, ("g", c, "c"), at(dc=1))

    def near(c):
        s = CHUNKS[c][0]
        for sign, dy, k, to in (("+", 3, 0, 1), ("-", 1, 1, 3)):
            arrived(cols.at[s, token_rows(dy), lanes(c)], "g", c, sign)
            push(cols.at[s, token_rows(dy, k), lanes(c)], ("gf", c), at(dy=to))
            push(cols.at[s, token_rows(dy), lanes(c)], ("g", c, "c"), at(dc=1))

    def far(c):
        s = CHUNKS[c][0]
        block = cols.at[s, token_rows(2), lanes(c)]
        arrived(block, "gf", c)
        if c < LAST:
            push(block, ("g", c, "c"), at(dc=1))
            arrived(cols.at[s, pl.ds(0, tokens // 2), lanes(c)], "g", c, "c")
        else:
            push(block, ("g", c, "cf"), at(dc=1))
            arrived(block, "g", c, "cf")

    def turn():
        for i, copy in enumerate(act_loads):
            copy.wait()
            for k in range(rows // 256):
                turned[pl.ds(k * 256, 256), pl.ds(i * share, share)] = (
                    plain[pl.ds(i * share, share), pl.ds(k * 256, 256)].T
                )
        peak[...] = jnp.zeros_like(peak)

    row_id = lax.broadcasted_iota(jnp.int32, peak.shape, 0)
    lane_id = lax.broadcasted_iota(jnp.int32, peak.shape, 1)

    def chip_tokens(dy):
        return pl.ds(pl.multiple_of(lax.rem(y + dy, RING) * 2 * share, 2 * share), 2 * share)

    def product(start, c, dy):
        here = chip_tokens(dy)
        return jnp.dot(
            turned[pl.ds(start, 256), here], cols[CHUNKS[c][0], here, lanes(c)], preferred_element_type=F32
        )

    def largest(c, t, i, value):
        s, halves = CHUNKS[c]
        top = peak[...]
        for k, h in enumerate(halves):
            for r in range(2):
                block = value[r * BLOCK:(r + 1) * BLOCK, k * BLOCK:(k + 1) * BLOCK]
                here = (row_id == t * (half // BLOCK) + i * 2 + r) & (lane_id == owner_of(s, h))
                top = jnp.where(here, jnp.max(jnp.abs(block), axis=(0, 1), keepdims=True), top)
        peak[...] = top

    def in_steps(t, step):
        def at_step(i, carry):
            step(i, pl.multiple_of(t * half + i * 256, 256))
            return carry

        lax.fori_loop(0, half // 256, at_step, 0)

    def mm(c, t):
        s = CHUNKS[c][0]

        def step(i, start):
            value = jnp.dot(turned[pl.ds(start, 256), :], cols[s, :, lanes(c)], preferred_element_type=F32)
            part[s, pl.ds(start, 256), lanes(c)] = value.astype(BF16)
            largest(c, t, i, value)

        in_steps(t, step)

    def mm_near(c, t):
        if t == 0:
            arrived(cols.at[CHUNKS[c][0], pl.ds(0, 3 * share), lanes(c)], "g", c, "c")

        def step(i, start):
            early[pl.ds(start, 256), :] = product(start, c, 0) + product(start, c, 1) + product(start, c, 3)

        in_steps(t, step)

    def mm_far(c, t):
        def step(i, start):
            value = early[pl.ds(start, 256), :] + product(start, c, 2)
            part[CHUNKS[c][0], pl.ds(start, 256), lanes(c)] = value.astype(BF16)
            early[pl.ds(start, 256), :] = value

        in_steps(t, step)

    def late(c, t):
        in_steps(t, lambda i, start: largest(c, t, i, early[pl.ds(start, 256), :]))

    def along(t, axis, delta):
        return at(dx=delta) if t == axis else at(dz=delta)

    def quarter_rows(t, delta=0):
        place = lax.rem((x if t == 0 else z) + delta, RING)
        return pl.ds(pl.multiple_of(t * half + place * quarter, quarter), quarter)

    def piece_of(t, delta=0):
        place = lax.rem((z if t == 0 else x) + delta, RING)
        return pl.ds(pl.multiple_of(place * piece, piece), piece)

    def piece_rows(t):
        a, b = (x, z) if t == 0 else (z, x)
        return pl.ds(pl.multiple_of(t * half + a * quarter + b * piece, piece), piece)

    def hand():
        for copy in state_loads:
            copy.wait()
        for i, ref in enumerate((w_in, f_in, s_in)):
            narrow[i] = ref[...].astype(BF16)
        for t in range(2):
            narrow_in[t, dp] = narrow[:, piece_rows(t), :]
            for delta in range(1, RING * RING):
                dz, dx = delta // RING, delta % RING
                a, b = lax.rem(x + dx, RING), lax.rem(z + dz, RING)
                if t == 1:
                    a, b = b, a
                here = pl.ds(pl.multiple_of(t * half + a * quarter + b * piece, piece), piece)
                push(narrow.at[:, here], ("hand",), at(dz=dz, dx=dx), dst=narrow_in.at[t, dp])

    def r1(c, t):
        s = CHUNKS[c][0]
        for delta in (1, 3, 2):
            push(
                part.at[s, quarter_rows(t, delta), lanes(c)], ("r1", c, t), along(t, 0, delta),
                dst=r1_in.at[s, t, delta - 1, :, lanes(c)],
            )

    def r1c(c, t):
        s = CHUNKS[c][0]
        arrived(r1_in.at[s, t, :, :, lanes(c)], "r1", c, t)
        total = part[s, quarter_rows(t), lanes(c)].astype(F32)
        for i in range(RING - 1):
            total = total + r1_in[s, t, i, :, lanes(c)].astype(F32)
        once[s, t, :, lanes(c)] = total.astype(BF16)
        for delta in (1, 3, 2):
            push(
                once.at[s, t, piece_of(t, delta), lanes(c)], ("r2", c, t), along(t, 1, delta),
                dst=r2_in.at[s, t, delta - 1, :, lanes(c)],
            )

    def u(c, t):
        s, halves = CHUNKS[c]
        if (c, t) == (0, 0):
            arrived(narrow_in.at[:, pl.ds(0, RING * RING - 1)], "hand")
        arrived(r2_in.at[s, t, :, :, lanes(c)], "r2", c, t)
        total = once[s, t, piece_of(t), lanes(c)].astype(F32)
        for i in range(RING - 1):
            total = total + r2_in[s, t, i, :, lanes(c)].astype(F32)
        total = total.astype(BF16)
        for k, h in enumerate(halves):
            owner = owner_of(s, h)
            block = total[:, k * BLOCK:(k + 1) * BLOCK]
            grads[s, t, h] = block
            state = [narrow_in[t, owner, i].astype(F32) for i in range(3)]
            gradient = block.astype(F32) * (1.0 / math.sqrt(token_count))
            held[s, piece_rows(t), h * BLOCK:(h + 1) * BLOCK] = adamw(*state, gradient)[0].astype(BF16)
        for delta in (1, 3, 2):
            push(held.at[s, piece_rows(t), lanes(c)], ("w1", c, t), along(t, 1, delta))
        for h in halves:
            owner = owner_of(s, h)
            source = grads.at[s, t, h]
            place = grad_in.at[piece_rows(t)]

            @pl.when(dp != owner)
            def _():
                push(source, ("grad",), (owner, tensor), dst=place)

            @pl.when(dp == owner)
            def _():
                place[...] = source[...]

    def w1(c, t):
        s = CHUNKS[c][0]
        arrived(held.at[s, pl.ds(0, 3 * piece), lanes(c)], "w1", c, t)
        for delta in (1, 3) if c < DIRECT else (2, 1, 3):
            push(
                held.at[s, quarter_rows(t), lanes(c)], ("w2" if delta != 2 else "w2f", c, t), along(t, 0, delta)
            )

    def w2(c, t):
        s = CHUNKS[c][0]
        arrived(held.at[s, pl.ds(0, 2 * quarter), lanes(c)], "w2", c, t)
        for k, to in ((0, 1), (1, 3)) if c < DIRECT else ():
            start = quarter_rows(t, RING - to).start + k * (quarter // 2)
            block = held.at[s, pl.ds(pl.multiple_of(start, quarter // 2), quarter // 2), lanes(c)]
            push(block, ("w2f", c, t), along(t, 0, to))

    def w3(c, t):
        arrived(held.at[CHUNKS[c][0], pl.ds(0, quarter), lanes(c)], "w2f", c, t)

    def states():
        arrived(grad_in.at[pl.ds(0, rows - 2 * piece)], "grad")
        gradient = grad_in[...].astype(F32) * (1.0 / math.sqrt(token_count))
        w_out[...], f_out[...], s_out[...] = adamw(w_in[...], f_in[...], s_in[...], gradient)

    def mx0():
        peak_x[...] = peak[...]
        for i in (1, 2, 3):
            push(peak_x, ("mx",), at(dx=i), dst=peak_in.at[i - 1])

    def mx1():
        arrived(peak_in.at[pl.ds(0, 3)], "mx")
        top = jnp.maximum(jnp.maximum(peak_in[0], peak_in[1]), jnp.maximum(peak_in[2], peak_x[...]))
        peak_z[...] = top
        for i in (1, 2, 3):
            push(peak_z, ("mz",), at(dz=i), dst=peak_in.at[i + 2])

    def mx2():
        arrived(peak_in.at[pl.ds(3, 3)], "mz")
        top = jnp.maximum(jnp.maximum(peak_in[3], peak_in[4]), jnp.maximum(peak_in[5], peak_z[...]))
        scales[...] = top[:, : scales.shape[1]] + 1e-06

    steps = {f.__name__: f for f in (own, near, far, hand, turn, mm, mm_near, mm_far, late, r1, r1c, u, w1, w2, w3, states, mx0, mx1, mx2)}
    for name, *args in schedule():
        steps[name](*args)

    sent(cols.at[:, pl.ds(0, 6 * share)], "g")
    sent(cols.at[:, pl.ds(0, share)], "gf")
    sent(narrow_in.at[:, pl.ds(0, RING * RING - 1)], "hand")
    sent(r1_in, "r1")
    sent(r2_in, "r2")
    sent(grad_in.at[pl.ds(0, rows - 2 * piece)], "grad")
    sent(held.at[:, pl.ds(0, 6 * piece)], "w1")
    sent(held.at[:, pl.ds(0, 4 * quarter)], "w2")
    sent(held.at[:, pl.ds(0, 2 * quarter)], "w2f")
    sent(peak_in.at[pl.ds(0, 3)], "mx")
    sent(peak_in.at[pl.ds(3, 3)], "mz")


def flush(*refs):
    count = (len(refs) - 1) // 2
    ins, outs, sems = refs[:count], refs[count:-1], refs[-1]
    copies = []

    def move(src, dst):
        copies.append(pltpu.make_async_copy(src, dst, sems.at[len(copies)]))
        copies[-1].start()

    for s in range(PAIRS):
        for h in range(2):
            j = s % 2 + 2 * h
            owner = j * RING + (j + s // 2) % RING
            move(ins[3].at[s, :, pl.ds(h * BLOCK, BLOCK)], outs[3].at[:, pl.ds(owner * BLOCK, BLOCK)])
    for i in (0, 1, 2, 4):
        move(ins[i], outs[i])
    for copy in copies:
        copy.wait()


def body(acts, cotangent, master, first_moment, second_moment):
    tokens, rows = acts.shape
    columns = cotangent.shape[1]
    state = pltpu.VMEM(master.shape, F32)
    anywhere = pl.BlockSpec(memory_space=pl.ANY)
    vmem = pltpu.VMEM
    quarter = rows // 2 // RING
    piece = quarter // RING
    scratch = [
        vmem((tokens, rows), BF16),
        vmem((rows, tokens), BF16),
        vmem((PAIRS, tokens, 2 * BLOCK), BF16),
        vmem((rows, len(CHUNKS[LAST][1]) * BLOCK), F32),
        vmem((PAIRS, rows, 2 * BLOCK), BF16),
        vmem((PAIRS, 2, RING - 1, quarter, 2 * BLOCK), BF16),
        vmem((PAIRS, 2, quarter, 2 * BLOCK), BF16),
        vmem((PAIRS, 2, RING - 1, piece, 2 * BLOCK), BF16),
        vmem((PAIRS, 2, 2, piece, BLOCK), BF16),
        vmem(master.shape, BF16),
    ]
    scratch += [vmem(master.shape, F32)] * 3
    scratch += [vmem((3,) + master.shape, BF16), vmem((2, RING * RING, 3, piece, BLOCK), BF16)]
    scratch += [vmem((8, BLOCK), F32)] * 3 + [vmem((6, 8, BLOCK), F32)]
    scratch += [
        pltpu.SemaphoreType.DMA((12,)),
        pltpu.SemaphoreType.DMA((128,)),
        pltpu.SemaphoreType.DMA((32,)),
    ]
    results = pl.pallas_call(
        functools.partial(kernel, tokens * lax.axis_size("dp")),
        out_shape=[
            state, state, state,
            vmem((PAIRS, rows, 2 * BLOCK), BF16),
            vmem((rows // BLOCK, columns // BLOCK), F32),
        ],
        in_specs=[anywhere] * 5,
        out_specs=[pl.BlockSpec(memory_space=pltpu.VMEM)] * 5,
        scratch_shapes=scratch,
        compiler_params=pltpu.CompilerParams(
            collective_id=0, has_side_effects=True, vmem_limit_bytes=50 * 2**20
        ),
    )(acts, cotangent, master, first_moment, second_moment)
    shapes = [a.shape for a in results]
    shapes[3] = (rows, columns)
    return pl.pallas_call(
        flush,
        out_shape=[jax.ShapeDtypeStruct(shape, a.dtype) for shape, a in zip(shapes, results)],
        in_specs=[anywhere] * len(results),
        out_specs=[anywhere] * len(results),
        scratch_shapes=[pltpu.SemaphoreType.DMA((2 * PAIRS + 4,))],
        compiler_params=pltpu.CompilerParams(vmem_limit_bytes=2**20),
    )(*results)


def solution(mesh):
    in_specs = (
        P("dp", "tensor"),
        P(("dp", "tensor"), None),
        P("tensor", "dp"),
        P("tensor", "dp"),
        P("tensor", "dp"),
    )
    out_specs = (
        P("tensor", "dp"),
        P("tensor", "dp"),
        P("tensor", "dp"),
        P("tensor", None),
        P("tensor", None),
    )
    return jax.shard_map(body, mesh=mesh, in_specs=in_specs, out_specs=out_specs, check_vma=False)
```

```python
import functools
import math

import jax
import jax.numpy as jnp
from jax import lax
from jax.experimental import pallas as pl
from jax.experimental.pallas import tpu as pltpu
from jax.sharding import PartitionSpec as P

MESH = pl.DeviceIdType.MESH
BLOCK = 128
RING = 4
PAIRS = 8
F32 = jnp.float32
BF16 = jnp.bfloat16


CHUNKS = [(s, (0, 1)) for s in range(PAIRS)]
LAST = len(CHUNKS) - 1
DIRECT = LAST


def schedule():
    ops = [("own", 0), ("own", 1), ("hand",), ("turn",)]

    def both(name, c):
        return [(name, c, 0), (name, c, 1)] if 0 <= c <= LAST else []

    for i in range(LAST + 1):
        ops.append(("near", i))
        if i + 2 <= LAST:
            ops.append(("own", i + 2))
        if i >= 1:
            ops.append(("far", i - 1))
            for t in range(2):
                ops += [("mm", i - 1, t), ("r1", i - 1, t)]
        ops += both("r1c", i - 2) + both("u", i - 3) + both("w1", i - 4) + both("w2", i - 5)
    ops += both("mm_near", LAST) + [("far", LAST)]
    for t in range(2):
        ops += [("mm_far", LAST, t), ("r1", LAST, t)]
    ops += both("late", LAST) + [("mx0",)]
    ops += both("r1c", LAST - 1) + both("u", LAST - 2) + both("w1", LAST - 3) + both("w2", LAST - 4)
    ops += both("r1c", LAST) + [("mx1",)] + both("u", LAST - 1) + both("w1", LAST - 2) + both("w2", LAST - 3)
    ops += both("u", LAST) + [("mx2",)] + both("w1", LAST - 1) + both("w2", LAST - 2)
    ops += both("w1", LAST) + both("w2", LAST - 1) + [("states",)] + both("w2", LAST)
    for c in range(LAST + 1):
        ops += both("w3", c)
    return ops


def adamw(master, first, second, gradient):
    f_new = 0.9 * first + 0.1 * gradient
    s_new = 0.95 * second + 0.05 * gradient * gradient
    f_hat = f_new / (1.0 - 0.9**10)
    s_hat = s_new / (1.0 - 0.95**10)
    w_new = master * (1.0 - 0.01 * 0.1) - 0.01 * f_hat / (jnp.sqrt(s_hat) + 1e-08)
    return w_new, f_new, s_new


def kernel(
    token_count,
    acts, cotangent, master, first, second,
    w_out, f_out, s_out, held, scales,
    plain, turned, cols, early, part, r1_in, once, r2_in, grads, grad_in,
    w_in, f_in, s_in, narrow, narrow_in,
    peak, peak_x, peak_z, peak_in,
    send, recv, local,
):
    dp, tensor = lax.axis_index("dp"), lax.axis_index("tensor")
    z, x = lax.div(dp, RING), lax.rem(dp, RING)
    y, core = lax.div(tensor, 2), lax.rem(tensor, 2)
    tokens, rows = plain.shape
    share = tokens // (2 * RING)
    half = rows // 2
    quarter = half // RING
    piece = quarter // RING

    def at(dz=0, dx=0, dy=0, dc=0):
        return (
            lax.rem(z + dz, RING) * RING + lax.rem(x + dx, RING),
            lax.rem(y + dy, RING) * 2 + lax.rem(core + dc, 2),
        )

    counts = {"send": 0, "recv": 0, "local": 0}
    names = {}

    def sem(kind, *key):
        if (kind, key) not in names:
            names[kind, key] = counts[kind]
            counts[kind] += 1
        return names[kind, key]

    def push(ref, key, device, dst=None):
        pltpu.make_async_remote_copy(
            src_ref=ref, dst_ref=ref if dst is None else dst,
            send_sem=send.at[sem("send", key[0])], recv_sem=recv.at[sem("recv", *key)],
            device_id=device, device_id_type=MESH,
        ).start()

    def arrived(ref, *key):
        pltpu.make_async_remote_copy(
            src_ref=ref, dst_ref=ref, send_sem=send.at[0], recv_sem=recv.at[sem("recv", *key)],
            device_id=at(dc=1), device_id_type=MESH,
        ).wait_recv()

    def sent(ref, kind, times=1):
        for _ in range(times):
            pltpu.make_async_remote_copy(
                src_ref=ref, dst_ref=ref, send_sem=send.at[sem("send", kind)], recv_sem=recv.at[0],
                device_id=at(dc=1), device_id_type=MESH,
            ).wait_send()

    def load(src, dst, *key):
        copy = pltpu.make_async_copy(src, dst, local.at[sem("local", *key)])
        copy.start()
        return copy

    def owner_of(s, h):
        d, j = s // 2, s % 2 + 2 * h
        return j * RING + (j + d) % RING

    barrier = pltpu.get_barrier_semaphore()
    partners = [at(dy=1), at(dy=3), at(dc=1)]
    partners += [at(dz=i // RING, dx=i % RING) for i in range(1, RING * RING)]
    for device in partners:
        pl.semaphore_signal(barrier, inc=1, device_id=device, device_id_type=MESH)

    mine = pl.ds(pl.multiple_of(tensor * share, share), share)
    own_loads = [
        [
            load(
                cotangent.at[:, pl.ds(owner_of(s, h) * BLOCK, BLOCK)],
                cols.at[s, mine, pl.ds(h * BLOCK, BLOCK)], "own", s, h,
            )
            for h in range(2)
        ]
        for s in range(PAIRS)
    ]
    state_loads = [
        load(a, b, "state", i) for i, (a, b) in enumerate(((master, w_in), (first, f_in), (second, s_in)))
    ]
    act_loads = [
        load(acts.at[pl.ds(i * share, share)], plain.at[pl.ds(i * share, share)], "acts", i)
        for i in range(2 * RING)
    ]

    pl.semaphore_wait(barrier, len(partners))

    def token_rows(dy, part_of=None):
        start = (lax.rem(y + dy, RING) * 2 + core) * share
        size = share
        if part_of is not None:
            size = share // 2
            start = start + part_of * size
        return pl.ds(pl.multiple_of(start, size), size)

    def lanes(c):
        return pl.ds(CHUNKS[c][1][0] * BLOCK, len(CHUNKS[c][1]) * BLOCK)

    def own(c):
        s, halves = CHUNKS[c]
        for h in halves:
            own_loads[s][h].wait()
        block = cols.at[s, token_rows(0), lanes(c)]
        push(block, ("g", c, "+"), at(dy=1))
        push(block, ("g", c, "-"), at(dy=3))
        push(block, ("g", c, "c"), at(dc=1))

    def near(c):
        s = CHUNKS[c][0]
        for sign, dy, k, to in (("+", 3, 0, 1), ("-", 1, 1, 3)):
            arrived(cols.at[s, token_rows(dy), lanes(c)], "g", c, sign)
            push(cols.at[s, token_rows(dy, k), lanes(c)], ("gf", c), at(dy=to))
            push(cols.at[s, token_rows(dy), lanes(c)], ("g", c, "c"), at(dc=1))

    def far(c):
        s = CHUNKS[c][0]
        block = cols.at[s, token_rows(2), lanes(c)]
        arrived(block, "gf", c)
        if c < LAST:
            push(block, ("g", c, "c"), at(dc=1))
            arrived(cols.at[s, pl.ds(0, tokens // 2), lanes(c)], "g", c, "c")
        else:
            push(block, ("g", c, "cf"), at(dc=1))
            arrived(block, "g", c, "cf")

    def turn():
        for i, copy in enumerate(act_loads):
            copy.wait()
            for k in range(rows // 256):
                turned[pl.ds(k * 256, 256), pl.ds(i * share, share)] = (
                    plain[pl.ds(i * share, share), pl.ds(k * 256, 256)].T
                )
        peak[...] = jnp.zeros_like(peak)

    row_id = lax.broadcasted_iota(jnp.int32, peak.shape, 0)
    lane_id = lax.broadcasted_iota(jnp.int32, peak.shape, 1)

    def chip_tokens(dy):
        return pl.ds(pl.multiple_of(lax.rem(y + dy, RING) * 2 * share, 2 * share), 2 * share)

    def product(start, c, dy):
        here = chip_tokens(dy)
        return jnp.dot(
            turned[pl.ds(start, 256), here], cols[CHUNKS[c][0], here, lanes(c)], preferred_element_type=F32
        )

    def largest(c, t, i, value):
        s, halves = CHUNKS[c]
        top = peak[...]
        for k, h in enumerate(halves):
            for r in range(2):
                block = value[r * BLOCK:(r + 1) * BLOCK, k * BLOCK:(k + 1) * BLOCK]
                here = (row_id == t * (half // BLOCK) + i * 2 + r) & (lane_id == owner_of(s, h))
                top = jnp.where(here, jnp.max(jnp.abs(block), axis=(0, 1), keepdims=True), top)
        peak[...] = top

    def in_steps(t, step):
        def at_step(i, carry):
            step(i, pl.multiple_of(t * half + i * 256, 256))
            return carry

        lax.fori_loop(0, half // 256, at_step, 0)

    def mm(c, t):
        s = CHUNKS[c][0]

        def step(i, start):
            value = jnp.dot(turned[pl.ds(start, 256), :], cols[s, :, lanes(c)], preferred_element_type=F32)
            part[s, pl.ds(start, 256), lanes(c)] = value.astype(BF16)
            largest(c, t, i, value)

        in_steps(t, step)

    def mm_near(c, t):
        if t == 0:
            arrived(cols.at[CHUNKS[c][0], pl.ds(0, 3 * share), lanes(c)], "g", c, "c")

        def step(i, start):
            early[pl.ds(start, 256), :] = product(start, c, 0) + product(start, c, 1) + product(start, c, 3)

        in_steps(t, step)

    def mm_far(c, t):
        def step(i, start):
            value = early[pl.ds(start, 256), :] + product(start, c, 2)
            part[CHUNKS[c][0], pl.ds(start, 256), lanes(c)] = value.astype(BF16)
            early[pl.ds(start, 256), :] = value

        in_steps(t, step)

    def late(c, t):
        in_steps(t, lambda i, start: largest(c, t, i, early[pl.ds(start, 256), :]))

    def along(t, axis, delta):
        return at(dx=delta) if t == axis else at(dz=delta)

    def quarter_rows(t, delta=0):
        place = lax.rem((x if t == 0 else z) + delta, RING)
        return pl.ds(pl.multiple_of(t * half + place * quarter, quarter), quarter)

    def piece_of(t, delta=0):
        place = lax.rem((z if t == 0 else x) + delta, RING)
        return pl.ds(pl.multiple_of(place * piece, piece), piece)

    def piece_rows(t):
        a, b = (x, z) if t == 0 else (z, x)
        return pl.ds(pl.multiple_of(t * half + a * quarter + b * piece, piece), piece)

    def hand():
        for copy in state_loads:
            copy.wait()
        for i, ref in enumerate((w_in, f_in, s_in)):
            narrow[i] = ref[...].astype(BF16)
        for t in range(2):
            narrow_in[t, dp] = narrow[:, piece_rows(t), :]
            for delta in range(1, RING * RING):
                dz, dx = delta // RING, delta % RING
                a, b = lax.rem(x + dx, RING), lax.rem(z + dz, RING)
                if t == 1:
                    a, b = b, a
                here = pl.ds(pl.multiple_of(t * half + a * quarter + b * piece, piece), piece)
                push(narrow.at[:, here], ("hand",), at(dz=dz, dx=dx), dst=narrow_in.at[t, dp])

    def r1(c, t):
        s = CHUNKS[c][0]
        for delta in (1, 3, 2):
            push(
                part.at[s, quarter_rows(t, delta), lanes(c)], ("r1", c, t), along(t, 0, delta),
                dst=r1_in.at[s, t, delta - 1, :, lanes(c)],
            )

    def r1c(c, t):
        s = CHUNKS[c][0]
        arrived(r1_in.at[s, t, :, :, lanes(c)], "r1", c, t)
        total = part[s, quarter_rows(t), lanes(c)].astype(F32)
        for i in range(RING - 1):
            total = total + r1_in[s, t, i, :, lanes(c)].astype(F32)
        once[s, t, :, lanes(c)] = total.astype(BF16)
        for delta in (1, 3, 2):
            push(
                once.at[s, t, piece_of(t, delta), lanes(c)], ("r2", c, t), along(t, 1, delta),
                dst=r2_in.at[s, t, delta - 1, :, lanes(c)],
            )

    def u(c, t):
        s, halves = CHUNKS[c]
        if (c, t) == (0, 0):
            arrived(narrow_in.at[:, pl.ds(0, RING * RING - 1)], "hand")
        arrived(r2_in.at[s, t, :, :, lanes(c)], "r2", c, t)
        total = once[s, t, piece_of(t), lanes(c)].astype(F32)
        for i in range(RING - 1):
            total = total + r2_in[s, t, i, :, lanes(c)].astype(F32)
        total = total.astype(BF16)
        for k, h in enumerate(halves):
            owner = owner_of(s, h)
            block = total[:, k * BLOCK:(k + 1) * BLOCK]
            grads[s, t, h] = block
            state = [narrow_in[t, owner, i].astype(F32) for i in range(3)]
            gradient = block.astype(F32) * (1.0 / math.sqrt(token_count))
            held[s, piece_rows(t), h * BLOCK:(h + 1) * BLOCK] = adamw(*state, gradient)[0].astype(BF16)
        for delta in (1, 3, 2):
            push(held.at[s, piece_rows(t), lanes(c)], ("w1", c, t), along(t, 1, delta))
        for h in halves:
            owner = owner_of(s, h)
            source = grads.at[s, t, h]
            place = grad_in.at[piece_rows(t)]

            @pl.when(dp != owner)
            def _():
                push(source, ("grad",), (owner, tensor), dst=place)

            @pl.when(dp == owner)
            def _():
                place[...] = source[...]

    def w1(c, t):
        s = CHUNKS[c][0]
        arrived(held.at[s, pl.ds(0, 3 * piece), lanes(c)], "w1", c, t)
        for delta in (1, 3) if c < DIRECT else (2, 1, 3):
            push(
                held.at[s, quarter_rows(t), lanes(c)], ("w2" if delta != 2 else "w2f", c, t), along(t, 0, delta)
            )

    def w2(c, t):
        s = CHUNKS[c][0]
        arrived(held.at[s, pl.ds(0, 2 * quarter), lanes(c)], "w2", c, t)
        for k, to in ((0, 1), (1, 3)) if c < DIRECT else ():
            start = quarter_rows(t, RING - to).start + k * (quarter // 2)
            block = held.at[s, pl.ds(pl.multiple_of(start, quarter // 2), quarter // 2), lanes(c)]
            push(block, ("w2f", c, t), along(t, 0, to))

    def w3(c, t):
        arrived(held.at[CHUNKS[c][0], pl.ds(0, quarter), lanes(c)], "w2f", c, t)

    def states():
        arrived(grad_in.at[pl.ds(0, rows - 2 * piece)], "grad")
        gradient = grad_in[...].astype(F32) * (1.0 / math.sqrt(token_count))
        w_out[...], f_out[...], s_out[...] = adamw(w_in[...], f_in[...], s_in[...], gradient)

    def mx0():
        peak_x[...] = peak[...]
        for i in (1, 2, 3):
            push(peak_x, ("mx",), at(dx=i), dst=peak_in.at[i - 1])

    def mx1():
        arrived(peak_in.at[pl.ds(0, 3)], "mx")
        top = jnp.maximum(jnp.maximum(peak_in[0], peak_in[1]), jnp.maximum(peak_in[2], peak_x[...]))
        peak_z[...] = top
        for i in (1, 2, 3):
            push(peak_z, ("mz",), at(dz=i), dst=peak_in.at[i + 2])

    def mx2():
        arrived(peak_in.at[pl.ds(3, 3)], "mz")
        top = jnp.maximum(jnp.maximum(peak_in[3], peak_in[4]), jnp.maximum(peak_in[5], peak_z[...]))
        scales[...] = top[:, : scales.shape[1]] + 1e-06

    steps = {f.__name__: f for f in (own, near, far, hand, turn, mm, mm_near, mm_far, late, r1, r1c, u, w1, w2, w3, states, mx0, mx1, mx2)}
    for name, *args in schedule():
        steps[name](*args)

    sent(cols.at[:, pl.ds(0, 6 * share)], "g")
    sent(cols.at[:, pl.ds(0, share)], "gf")
    sent(narrow_in.at[:, pl.ds(0, RING * RING - 1)], "hand")
    sent(r1_in, "r1")
    sent(r2_in, "r2")
    sent(grad_in.at[pl.ds(0, rows - 2 * piece)], "grad")
    sent(held.at[:, pl.ds(0, 6 * piece)], "w1")
    sent(held.at[:, pl.ds(0, 4 * quarter)], "w2")
    sent(held.at[:, pl.ds(0, 2 * quarter)], "w2f")
    sent(peak_in.at[pl.ds(0, 3)], "mx")
    sent(peak_in.at[pl.ds(3, 3)], "mz")


def flush(*refs):
    count = (len(refs) - 1) // 2
    ins, outs, sems = refs[:count], refs[count:-1], refs[-1]
    copies = []

    def move(src, dst, cuts=1):
        size = dst.shape[0] // cuts
        for i in range(cuts):
            here = pl.ds(i * size, size)
            copies.append(pltpu.make_async_copy(src.at[here], dst.at[here], sems.at[len(copies)]))
            copies[-1].start()

    for s in range(PAIRS):
        for h in range(2):
            j = s % 2 + 2 * h
            owner = j * RING + (j + s // 2) % RING
            move(ins[3].at[s, :, pl.ds(h * BLOCK, BLOCK)], outs[3].at[:, pl.ds(owner * BLOCK, BLOCK)], 2)
    for i in (0, 1, 2):
        move(ins[i], outs[i], 4)
    move(ins[4], outs[4])
    for copy in copies:
        copy.wait()


def body(acts, cotangent, master, first_moment, second_moment):
    tokens, rows = acts.shape
    columns = cotangent.shape[1]
    state = pltpu.VMEM(master.shape, F32)
    anywhere = pl.BlockSpec(memory_space=pl.ANY)
    vmem = pltpu.VMEM
    quarter = rows // 2 // RING
    piece = quarter // RING
    scratch = [
        vmem((tokens, rows), BF16),
        vmem((rows, tokens), BF16),
        vmem((PAIRS, tokens, 2 * BLOCK), BF16),
        vmem((rows, len(CHUNKS[LAST][1]) * BLOCK), F32),
        vmem((PAIRS, rows, 2 * BLOCK), BF16),
        vmem((PAIRS, 2, RING - 1, quarter, 2 * BLOCK), BF16),
        vmem((PAIRS, 2, quarter, 2 * BLOCK), BF16),
        vmem((PAIRS, 2, RING - 1, piece, 2 * BLOCK), BF16),
        vmem((PAIRS, 2, 2, piece, BLOCK), BF16),
        vmem(master.shape, BF16),
    ]
    scratch += [vmem(master.shape, F32)] * 3
    scratch += [vmem((3,) + master.shape, BF16), vmem((2, RING * RING, 3, piece, BLOCK), BF16)]
    scratch += [vmem((8, BLOCK), F32)] * 3 + [vmem((6, 8, BLOCK), F32)]
    scratch += [
        pltpu.SemaphoreType.DMA((12,)),
        pltpu.SemaphoreType.DMA((128,)),
        pltpu.SemaphoreType.DMA((32,)),
    ]
    results = pl.pallas_call(
        functools.partial(kernel, tokens * lax.axis_size("dp")),
        out_shape=[
            state, state, state,
            vmem((PAIRS, rows, 2 * BLOCK), BF16),
            vmem((rows // BLOCK, columns // BLOCK), F32),
        ],
        in_specs=[anywhere] * 5,
        out_specs=[pl.BlockSpec(memory_space=pltpu.VMEM)] * 5,
        scratch_shapes=scratch,
        compiler_params=pltpu.CompilerParams(
            collective_id=0, has_side_effects=True, vmem_limit_bytes=50 * 2**20
        ),
    )(acts, cotangent, master, first_moment, second_moment)
    shapes = [a.shape for a in results]
    shapes[3] = (rows, columns)
    return pl.pallas_call(
        flush,
        out_shape=[jax.ShapeDtypeStruct(shape, a.dtype) for shape, a in zip(shapes, results)],
        in_specs=[anywhere] * len(results),
        out_specs=[anywhere] * len(results),
        scratch_shapes=[pltpu.SemaphoreType.DMA((4 * PAIRS + 13,))],
        compiler_params=pltpu.CompilerParams(vmem_limit_bytes=2**20),
    )(*results)


def solution(mesh):
    in_specs = (
        P("dp", "tensor"),
        P(("dp", "tensor"), None),
        P("tensor", "dp"),
        P("tensor", "dp"),
        P("tensor", "dp"),
    )
    out_specs = (
        P("tensor", "dp"),
        P("tensor", "dp"),
        P("tensor", "dp"),
        P("tensor", None),
        P("tensor", None),
    )
    return jax.shard_map(body, mesh=mesh, in_specs=in_specs, out_specs=out_specs, check_vma=False)
```
